256 devices in a mesh: replica: 64 (over x, y_hi, z), fsdp: 4 (over y_lo, core).
Axes of the slice: x: 4, y: 4 (y_hi: 2, y_lo: 2; y = y_hi * 2 + y_lo), z: 8, core: 2. Of those that a mesh axis runs over, the one named last changes fastest.
Arguments:
- tokens: bfloat16 [32768, 8192], P(('replica', 'fsdp')), may hold values from -6 to 6
- norm_gain: float32 [8192], replicated, may hold values from 0.25 to 1.75
- key_weight: bfloat16 [64, 8192, 512], P('replica', 'fsdp'), may hold values from -6 to 6
- key_cotangent: bfloat16 [32768, 512], P(('replica', 'fsdp')), may hold values from -6 to 6
- fragment_local: bfloat16 [64, 8192, 512], P('replica', 'fsdp'), may hold values from -16 to 16
- fragment_global: float32 [4, 2048, 512], P('fsdp', 'replica'), may hold values from -6 to 6
- outer_moment: float32 [4, 2048, 512], P('fsdp', 'replica'), may hold values from -4 to 4
Outputs:
- key_out: bfloat16 [32768, 512], P(('replica', 'fsdp'))
- input_grad: bfloat16 [32768, 8192], P(('replica', 'fsdp'))
- key_weight_new: bfloat16 [64, 8192, 512], P('replica', 'fsdp')
- fragment_mixed: bfloat16 [64, 8192, 512], P('replica', 'fsdp')
- moment_new: float32 [4, 2048, 512], P('fsdp', 'replica')
- global_new: float32 [4, 2048, 512], P('fsdp', 'replica')
The draws below stay inside these ranges and needn't reach their ends.
All inputs are finite; a program needn't handle non-finite values.
Results may differ from the reference program's by a relative error of at most 0.014.
Values may be sent and summed in bfloat16 or wider, within the bound.
A program may use at most 128 MiB of HBM per device.

```python
from functools import partial
import jax
import jax.numpy as jnp
from jax import lax

D = 8192
TOK_DEV = 128
KVW = 512
TOK_REP = 512
TOKENS = 32768
N_REPLICA = 64
N_FSDP = 4


def spiked(entries, rng, source, target, shards_of, factor):
    owner, partner = [(jnp.arange(entries.shape[axis_at]) // (entries.shape[axis_at] // shards_of)).reshape([-1 if axis == axis_at else 1 for axis in range(entries.ndim)]) for axis_at in (source, target)]
    chosen = jax.random.permutation(rng, shards_of)[partner]
    strong = (owner == chosen) | (owner == (partner + shards_of // 2) % shards_of)
    return jnp.where(strong, factor * entries, entries)


def level_of(stream_key, extent, pieces, least, high):
    def one(axis_at, parts):
        steps = jax.random.uniform(jax.random.fold_in(jax.random.fold_in(stream_key, 6), axis_at), (parts,), jnp.float32, least / len(pieces), high / len(pieces))
        return jnp.repeat(jnp.exp(steps), extent[axis_at] // parts).reshape((-1,) + (1,) * (len(extent) - axis_at - 1))

    gain = one(*pieces[0])
    for cut in pieces[1:]:
        gain = gain * one(*cut)
    return gain


def noise(own_key, dims, scale, bound, cuts=(), kind=jnp.bfloat16):
    array = jax.random.normal(own_key, dims, jnp.float32) * scale
    if len(cuts) > 0:
        array = level_of(own_key, dims, cuts, -0.22, 0.18) * array
    return jnp.clip(array, min=-bound, max=bound).astype(kind)


def heavy_noise(own_key, extent, deviation, limit, cuts, heavy, held_as=jnp.bfloat16):
    values = deviation * jax.random.normal(own_key, extent, jnp.float32)
    if cuts:
        values = values * level_of(own_key, extent, cuts, -0.22, 0.18)
    return jnp.clip(spiked(values, jax.random.fold_in(own_key, 3), *heavy), -limit, limit).astype(held_as)


def setup_inputs(seed: int = 0) -> dict:
    keys = jax.random.split(jax.random.key(seed), 8)
    tokens = noise(keys[0], (TOKENS, D), 1.0, 6.0, ((0, 256),))
    norm_gain = jnp.clip(1.0 + 0.15 * jax.random.normal(keys[1], (D,), jnp.float32), 0.25, 1.75)
    key_weight = noise(keys[2], (N_REPLICA, D, KVW), 1.0, 6.0, ((0, 64), (1, 4)))
    key_cotangent = noise(keys[3], (TOKENS, KVW), 1.0, 6.0, ((0, 256),))
    fragment_local = heavy_noise(keys[4], (N_REPLICA, D, KVW), 1.0, 16.0, ((0, 64), (1, 4)), (0, 1, 64, 4.0))
    fragment_global = noise(keys[5], (N_FSDP, D // N_FSDP, KVW), 1.0, 6.0, ((0, 4), (1, 64)), jnp.float32)
    outer_moment = noise(keys[6], (N_FSDP, D // N_FSDP, KVW), 0.5, 4.0, ((0, 4), (1, 64)), jnp.float32)
    return {"tokens": tokens, "norm_gain": norm_gain, "key_weight": key_weight, "key_cotangent": key_cotangent, "fragment_local": fragment_local, "fragment_global": fragment_global, "outer_moment": outer_moment}


norm_eps = 1e-05
inner_rate = 1.0
outer_rate = 0.7
momentum_decay = 0.9
mix_keep = 0.5

def inner_replica(gain_vector, operands):
    tokens_rep, weight_rep, cotangent_rep = operands
    factor = D ** (-0.5)
    feature = tokens_rep.astype(jnp.float32)
    inverse = lax.rsqrt(lax.optimization_barrier(jnp.mean(feature * feature, axis=1, keepdims=True)) + norm_eps)
    scaled = feature * inverse
    normed = (scaled * gain_vector).astype(jnp.bfloat16)
    key_sums = jnp.dot(normed, weight_rep, preferred_element_type=jnp.float32)
    key_out = (factor * key_sums).astype(jnp.bfloat16)
    back_grad = factor * lax.dot_general(cotangent_rep, weight_rep, (((1,), (1,)), ((), ())), preferred_element_type=jnp.float32)
    gain_back = gain_vector * back_grad
    input_grad = (inverse * (gain_back - scaled * lax.optimization_barrier(jnp.mean(scaled * gain_back, axis=1, keepdims=True)))).astype(jnp.bfloat16)
    group_norm = normed.reshape(N_FSDP, TOK_DEV, D)
    group_cot = cotangent_rep.reshape(N_FSDP, TOK_DEV, KVW)

    def group_term(pair):
        return (factor * lax.dot_general(pair[0], pair[1], (((0,), (0,)), ((), ())), preferred_element_type=jnp.float32)).astype(jnp.bfloat16)
    partial_terms = lax.optimization_barrier(lax.map(group_term, (group_norm, group_cot)))
    weight_grad = lax.optimization_barrier(jnp.sum(partial_terms.astype(jnp.float32), axis=0))
    weight_new = (weight_rep.astype(jnp.float32) - inner_rate * weight_grad).astype(jnp.bfloat16)
    return (key_out, input_grad, weight_new)

def reference(tokens, norm_gain, key_weight, key_cotangent, fragment_local, fragment_global, outer_moment):
    token_blocks = tokens.reshape(N_REPLICA, TOK_REP, D)
    cot_blocks = key_cotangent.reshape(N_REPLICA, TOK_REP, KVW)
    key_out, input_grad, key_weight_new = lax.map(partial(inner_replica, norm_gain), (token_blocks, key_weight, cot_blocks))
    summed = lax.optimization_barrier(jnp.sum(fragment_local, axis=0, dtype=jnp.float32))
    global_flat = fragment_global.reshape(D, KVW)
    moment_flat = outer_moment.reshape(D, KVW)
    outer_grad = global_flat - summed / N_REPLICA
    moment_new = momentum_decay * moment_flat + outer_grad
    global_new = global_flat - outer_rate * (outer_grad + momentum_decay * moment_new)
    global_round = lax.optimization_barrier(global_new.astype(jnp.bfloat16)).astype(jnp.float32)

    def mix_one(local_rep):
        return (mix_keep * local_rep.astype(jnp.float32) + (1.0 - mix_keep) * global_round).astype(jnp.bfloat16)
    fragment_mixed = lax.map(mix_one, fragment_local)
    return (key_out.reshape(TOKENS, KVW), input_grad.reshape(TOKENS, D), key_weight_new, fragment_mixed, moment_new.reshape(N_FSDP, D // N_FSDP, KVW), global_new.reshape(N_FSDP, D // N_FSDP, KVW))
```

```python
import jax
import jax.numpy as jnp
from jax import lax
from jax.experimental import pallas as pl
from jax.experimental.pallas import tpu as pltpu
from jax.sharding import PartitionSpec as P

norm_eps = 1e-05
inner_rate = 1.0
outer_rate = 0.7
momentum_decay = 0.9
mix_keep = 0.5

MESH = pl.DeviceIdType.MESH
NX, NH, NZ, NF = 4, 2, 8, 4
REPLICAS = NX * NH * NZ
TOK, D, KV = 128, 8192, 512
COLS = D // NF
SHARE = COLS // REPLICAS
XB = COLS // NX
K = 4
KC = KV // K
PARTS = 4
PR = TOK // PARTS
SLAB = 512
FACTOR = D ** (-0.5)
N_COPIES = 128
N_LOADS = 16
f32, bf16 = jnp.float32, jnp.bfloat16


def kernel(
    tokens,
    gain_in,
    weight_in,
    cot_in,
    frag_in,
    global_in,
    moment_in,
    key_out,
    input_grad,
    weight_new,
    mixed,
    moment_new,
    global_new,
    tok,
    gain,
    weight,
    frag,
    glob,
    moment,
    cot,
    nin,
    nout,
    inv_s,
    bout,
    bin_,
    kp,
    kp1,
    kx,
    ksend,
    kc,
    xr,
    s1,
    zr,
    s2,
    yr,
    gx,
    send_sem,
    recv_sem,
    load_sem,
):
    r = lax.axis_index("replica")
    f = lax.axis_index("fsdp")
    x, yh, z = r // (NH * NZ), (r // NZ) % NH, r % NZ
    yl, core = f // 2, f % 2

    def fsdp_peer(q):
        a = 1 - yl if q & 2 else yl
        b = 1 - core if q & 1 else core
        return a * 2 + b

    def x_peer(d):
        return (((x + d) % NX) * NH + yh) * NZ + z, f

    def z_peer(d):
        return (x * NH + yh) * NZ + (z + d) % NZ, f

    y_peer = ((x * NH + (1 - yh)) * NZ + z, f)
    f_peer = {q: (r, fsdp_peer(q)) for q in (1, 2, 3)}

    loads = []

    def load(src, dst):
        copy = pltpu.make_async_copy(src, dst, load_sem.at[len(loads)])
        copy.start()
        loads.append(copy)
        return copy

    def block_cols(q):
        return pl.ds(pl.multiple_of((fsdp_peer(q) if q else f) * COLS, COLS), COLS)

    load_tok = [load(tokens.at[:, block_cols(q)], tok.at[q]) for q in range(NF)]
    load_gain = [load(gain_in.at[:, block_cols(q)], gain.at[q]) for q in range(NF)]
    load_cot = load(cot_in, cot.at[0])
    load_weight = load(weight_in.at[0], weight)
    load_frag = load(frag_in.at[0], frag)
    load_outer = [load(global_in.at[0], glob), load(moment_in.at[0], moment)]

    barrier = pltpu.get_barrier_semaphore()
    peers = (
        [f_peer[q] for q in (1, 2, 3)]
        + [x_peer(d) for d in range(1, NX)]
        + [z_peer(d) for d in range(1, NZ)]
        + [y_peer]
    )
    for peer in peers:
        pl.semaphore_signal(barrier, 1, device_id=peer, device_id_type=MESH)

    copies = []

    def remote(src, dst, device):
        i = len(copies)
        copy = pltpu.make_async_remote_copy(
            src, dst, send_sem.at[i], recv_sem.at[i], device_id=device, device_id_type=MESH
        )
        copy.start()
        copies.append(copy)
        return copy

    def rows_of(c):
        return pl.ds(c * PR, PR)

    def fold(v):
        return v[:, :128] + v[:, 128:256] + v[:, 256:384] + v[:, 384:]

    def normalise(c):
        rows = rows_of(c)

        def square(q, acc):
            for s in range(COLS // SLAB):
                v = tok[q, rows, pl.ds(s * SLAB, SLAB)].astype(f32)
                acc = acc + fold(v * v)
            return acc

        acc = lax.fori_loop(0, NF, square, jnp.zeros((PR, 128), f32))
        inv = lax.rsqrt(jnp.sum(acc, axis=1, keepdims=True) * (1.0 / D) + norm_eps)
        inv_s[rows, :] = jnp.broadcast_to(inv, (PR, 128))

        def scale(q, dst):
            for s in range(COLS // SLAB):
                lanes = pl.ds(s * SLAB, SLAB)
                v = tok[q, rows, lanes].astype(f32)
                dst[q, rows, lanes] = (v * inv * gain[q, :, lanes]).astype(bf16)

        scale(0, nin)

        def others(q, _):
            scale(q, nout)
            return 0

        lax.fori_loop(1, NF, others, 0)

    def send_normed(c, q):
        return remote(nout.at[q, rows_of(c)], nin.at[q, rows_of(c)], f_peer[q])

    def back_products():
        left = cot[...].reshape(NF * TOK, KV)

        def tile(t, _):
            rows = pl.ds(pl.multiple_of(t * 256, 256), 256)
            res = lax.dot_general(
                left, weight[rows, :], (((1,), (1,)), ((), ())), preferred_element_type=f32
            )
            res = (FACTOR * res).astype(bf16)
            bin_[0, :, rows] = res[:TOK]
            for q in range(1, NF):
                bout[q, :, rows] = res[q * TOK : (q + 1) * TOK]
            return 0

        lax.fori_loop(0, COLS // 256, tile, 0)

    def send_back(c, q):
        return remote(bout.at[q, rows_of(c)], bin_.at[q, rows_of(c)], f_peer[q])

    def key_products():
        left = nin[...].reshape(NF * TOK, COLS)
        for n in range(2):
            lanes = pl.ds(n * 256, 256)
            res = jnp.dot(left, weight[:, lanes], preferred_element_type=f32)
            for q in range(NF):
                kp[q, :, lanes] = res[q * TOK : (q + 1) * TOK]

    def weight_products():
        right = cot[...].reshape(NF * TOK, KV)

        def tile(t, _):
            rows = pl.ds(pl.multiple_of(t * 256, 256), 256)
            left = nin[:, :, rows].reshape(NF * TOK, 256)
            res = lax.dot_general(
                left, right, (((0,), (0,)), ((), ())), preferred_element_type=f32
            )
            weight_new[0, rows, :] = (
                weight[rows, :].astype(f32) - inner_rate * (FACTOR * res)
            ).astype(bf16)
            return 0

        lax.fori_loop(0, COLS // 256, tile, 0)

    def finish_tokens(c):
        rows = rows_of(c)
        inv = inv_s[rows, :][:, :1]

        def project(q, acc):
            for s in range(COLS // SLAB):
                lanes = pl.ds(s * SLAB, SLAB)
                scaled = tok[q, rows, lanes].astype(f32) * inv
                gain_back = gain[q, :, lanes] * bin_[q, rows, lanes].astype(f32)
                acc = acc + fold(scaled * gain_back)
            return acc

        acc = lax.fori_loop(0, NF, project, jnp.zeros((PR, 128), f32))
        mean = jnp.sum(acc, axis=1, keepdims=True) * (1.0 / D)
        for q in range(NF):
            owner = fsdp_peer(q) if q else f
            for s in range(COLS // SLAB):
                lanes = pl.ds(s * SLAB, SLAB)
                scaled = tok[q, rows, lanes].astype(f32) * inv
                gain_back = gain[q, :, lanes] * bin_[q, rows, lanes].astype(f32)
                out = pl.ds(pl.multiple_of(owner * COLS + s * SLAB, SLAB), SLAB)
                input_grad[rows, out] = (inv * (gain_back - scaled * mean)).astype(bf16)

    def x_scatter(k):
        return [
            remote(
                frag_in.at[
                    0,
                    pl.ds(pl.multiple_of(((x + d) % NX) * XB, XB), XB),
                    pl.ds(k * KC, KC),
                ],
                xr.at[k, d - 1],
                x_peer(d),
            )
            for d in range(1, NX)
        ]

    def x_sum(k):
        lanes = pl.ds(k * KC, KC)
        for h in range(NH):
            base = ((yh + h) % NH) * (NZ * SHARE)

            def one(zi, _):
                at = base + zi * SHARE
                own = pl.ds(pl.multiple_of(x * XB + at, SHARE), SHARE)
                rows = pl.ds(pl.multiple_of(at, SHARE), SHARE)
                total = frag[own, lanes].astype(f32)
                for d in range(NX - 1):
                    total = total + xr[k, d, rows, :].astype(f32)
                s1[k, zi, h] = total
                return 0

            lax.fori_loop(0, NZ, one, 0)

    def z_scatter(k):
        return [
            remote(s1.at[k, (z + d) % NZ], zr.at[k, d - 1], z_peer(d)) for d in range(1, NZ)
        ]

    def z_sum(k):
        total = s1[k, z]
        for d in range(NZ - 1):
            total = total + zr[k, d]
        s2[k] = total

    def y_scatter(k):
        return remote(s2.at[k, 1], yr.at[k], y_peer)

    def update(k):
        lanes = pl.ds(k * KC, KC)
        mean = (s2[k, 0] + yr[k]) * (1.0 / REPLICAS)
        g = glob[:, lanes]
        outer_grad = g - mean
        m = momentum_decay * moment[:, lanes] + outer_grad
        g = g - outer_rate * (outer_grad + momentum_decay * m)
        moment_new[0, :, lanes] = m
        global_new[0, :, lanes] = g
        gx[0, k, 0, 0] = g.astype(bf16)

    def y_gather(k):
        return remote(gx.at[0, k, 0, 0], gx.at[0, k, 0, 1], y_peer)

    def z_gather(k):
        return [remote(gx.at[0, k, 0], gx.at[0, k, d], z_peer(d)) for d in range(1, NZ)]

    def x_gather(k):
        return [remote(gx.at[0, k], gx.at[e, k], x_peer(e)) for e in range(1, NX)]

    def mix(k, e):
        lanes = pl.ds(k * KC, KC)
        xi = (x + NX - e) % NX
        for h in range(NH):
            base = xi * XB + ((yh + h) % NH) * (NZ * SHARE)

            def one(d, _):
                at = base + ((z + NZ - d) % NZ) * SHARE
                rows = pl.ds(pl.multiple_of(at, SHARE), SHARE)
                mixed[0, rows, lanes] = (
                    mix_keep * frag[rows, lanes].astype(f32)
                    + (1.0 - mix_keep) * gx[e, k, d, h].astype(f32)
                ).astype(bf16)
                return 0

            lax.fori_loop(0, NZ, one, 0)

    def arrive(group):
        for copy in group if isinstance(group, list) else [group]:
            copy.wait_recv()

    for copy in load_tok + load_gain:
        copy.wait()
    normalise(0)
    pl.semaphore_wait(barrier, len(peers))
    cot1 = remote(cot_in, cot.at[1], f_peer[1])
    cot2 = remote(cot_in, cot.at[2], f_peer[2])
    xs = [x_scatter(0), x_scatter(1)]
    nq = {}
    bq = {}
    for q in (2, 3, 1):
        nq[0, q] = send_normed(0, q)
    xs += [x_scatter(2), x_scatter(3)]
    for c in range(1, PARTS):
        normalise(c)
        nq[c, 1] = send_normed(c, 1)
    arrive(cot2)
    cot3 = remote(cot.at[2], cot.at[3], f_peer[1])
    nq[1, 2] = send_normed(1, 2)

    load_frag.wait()
    arrive(xs[0])
    x_sum(0)
    zs = [z_scatter(0)]
    nq[1, 3] = send_normed(1, 3)
    nq[2, 2] = send_normed(2, 2)
    load_cot.wait()
    load_weight.wait()
    arrive(cot1)
    arrive(cot3)
    back_products()
    for c in range(PARTS):
        bq[c, 1] = send_back(c, 1)

    arrive(xs[1])
    x_sum(1)
    zs.append(z_scatter(1))
    arrive(zs[0])
    z_sum(0)
    ys = [y_scatter(0)]
    nq[2, 3] = send_normed(2, 3)
    nq[3, 2] = send_normed(3, 2)
    for copy in load_outer:
        copy.wait()

    arrive(xs[2])
    x_sum(2)
    zs.append(z_scatter(2))
    arrive(zs[1])
    z_sum(1)
    ys.append(y_scatter(1))
    arrive(ys[0])
    update(0)
    yg = [y_gather(0)]
    nq[3, 3] = send_normed(3, 3)
    bq[0, 2] = send_back(0, 2)

    arrive(xs[3])
    x_sum(3)
    zs.append(z_scatter(3))
    arrive(zs[2])
    z_sum(2)
    ys.append(y_scatter(2))
    arrive(ys[1])
    update(1)
    yg.append(y_gather(1))
    arrive(yg[0])
    zg = [z_gather(0)]
    bq[0, 3] = send_back(0, 3)
    bq[1, 2] = send_back(1, 2)

    arrive(zs[3])
    z_sum(3)
    ys.append(y_scatter(3))
    arrive(ys[2])
    update(2)
    yg.append(y_gather(2))
    arrive(yg[1])
    zg.append(z_gather(1))
    arrive(zg[0])
    xg = [x_gather(0)]
    bq[1, 3] = send_back(1, 3)
    bq[2, 2] = send_back(2, 2)
    for c in range(PARTS):
        for q in (1, 2, 3):
            arrive(nq[c, q])
    key_products()
    k3 = remote(kp.at[3], kx, f_peer[1])
    k1 = remote(kp.at[1], kp1, f_peer[1])

    arrive(ys[3])
    update(3)
    yg.append(y_gather(3))
    arrive(yg[2])
    zg.append(z_gather(2))
    arrive(zg[1])
    xg.append(x_gather(1))
    arrive(k3)
    ksend[...] = (FACTOR * (kp[2] + kx[...])).astype(bf16)
    k2 = remote(ksend, kc, f_peer[2])
    bq[2, 3] = send_back(2, 3)
    arrive(yg[3])
    zg.append(z_gather(3))
    bq[3, 2] = send_back(3, 2)
    bq[3, 3] = send_back(3, 3)
    arrive(zg[2])
    xg.append(x_gather(2))
    arrive(zg[3])
    xg.append(x_gather(3))
    weight_products()

    for k in range(K):
        mix(k, 0)
    for k in range(K):
        for c in range(PARTS):
            if c == k:
                for q in (1, 2, 3):
                    arrive(bq[c, q])
                finish_tokens(c)
        arrive(xg[k])
        for e in range(1, NX):
            mix(k, e)
        if k == 1:
            arrive(k1)
            arrive(k2)
            key_out[...] = (FACTOR * (kp[0] + kp1[...]) + kc[...].astype(f32)).astype(bf16)
    for copy in copies:
        copy.wait_send()


def local(
    tokens, norm_gain, key_weight, key_cotangent, fragment_local, fragment_global, outer_moment
):
    any_space = pl.BlockSpec(memory_space=pl.ANY)
    vmem = pl.BlockSpec(memory_space=pltpu.VMEM)
    return pl.pallas_call(
        kernel,
        name="diloco_step",
        out_shape=(
            jax.ShapeDtypeStruct((TOK, KV), bf16),
            jax.ShapeDtypeStruct((TOK, D), bf16),
            jax.ShapeDtypeStruct((1, COLS, KV), bf16),
            jax.ShapeDtypeStruct((1, COLS, KV), bf16),
            jax.ShapeDtypeStruct((1, SHARE, KV), f32),
            jax.ShapeDtypeStruct((1, SHARE, KV), f32),
        ),
        in_specs=[any_space] * 7,
        out_specs=(vmem,) * 6,
        scratch_shapes=[
            pltpu.VMEM((NF, TOK, COLS), bf16),
            pltpu.VMEM((NF, 1, COLS), f32),
            pltpu.VMEM((COLS, KV), bf16),
            pltpu.VMEM((COLS, KV), bf16),
            pltpu.VMEM((SHARE, KV), f32),
            pltpu.VMEM((SHARE, KV), f32),
            pltpu.VMEM((NF, TOK, KV), bf16),
            pltpu.VMEM((NF, TOK, COLS), bf16),
            pltpu.VMEM((NF, TOK, COLS), bf16),
            pltpu.VMEM((TOK, 128), f32),
            pltpu.VMEM((NF, TOK, COLS), bf16),
            pltpu.VMEM((NF, TOK, COLS), bf16),
            pltpu.VMEM((NF, TOK, KV), f32),
            pltpu.VMEM((TOK, KV), f32),
            pltpu.VMEM((TOK, KV), f32),
            pltpu.VMEM((TOK, KV), bf16),
            pltpu.VMEM((TOK, KV), bf16),
            pltpu.VMEM((K, NX - 1, XB, KC), bf16),
            pltpu.VMEM((K, NZ, NH, SHARE, KC), f32),
            pltpu.VMEM((K, NZ - 1, NH, SHARE, KC), f32),
            pltpu.VMEM((K, NH, SHARE, KC), f32),
            pltpu.VMEM((K, SHARE, KC), f32),
            pltpu.VMEM((NX, K, NZ, NH, SHARE, KC), bf16),
            pltpu.SemaphoreType.DMA((N_COPIES,)),
            pltpu.SemaphoreType.DMA((N_COPIES,)),
            pltpu.SemaphoreType.DMA((N_LOADS,)),
        ],
        compiler_params=pltpu.CompilerParams(
            collective_id=0, has_side_effects=True, vmem_limit_bytes=50 << 20
        ),
    )(
        tokens,
        norm_gain[None],
        key_weight,
        key_cotangent,
        fragment_local,
        fragment_global,
        outer_moment,
    )


def solution(mesh):
    return jax.shard_map(
        local,
        mesh=mesh,
        in_specs=(
            P(("replica", "fsdp"), None),
            P(),
            P("replica", "fsdp", None),
            P(("replica", "fsdp"), None),
            P("replica", "fsdp", None),
            P("fsdp", "replica", None),
            P("fsdp", "replica", None),
        ),
        out_specs=(
            P(("replica", "fsdp"), None),
            P(("replica", "fsdp"), None),
            P("replica", "fsdp", None),
            P("replica", "fsdp", None),
            P("fsdp", "replica", None),
            P("fsdp", "replica", None),
        ),
        check_vma=False,
    )
```

```python
import jax
import jax.numpy as jnp
from jax import lax
from jax.experimental import pallas as pl
from jax.experimental.pallas import tpu as pltpu
from jax.sharding import PartitionSpec as P

norm_eps = 1e-05
inner_rate = 1.0
outer_rate = 0.7
momentum_decay = 0.9
mix_keep = 0.5

MESH = pl.DeviceIdType.MESH
NX, NH, NZ, NF = 4, 2, 8, 4
REPLICAS = NX * NH * NZ
TOK, D, KV = 128, 8192, 512
COLS = D // NF
SHARE = COLS // REPLICAS
XB = COLS // NX
K = 4
KC = KV // K
PARTS = 4
PR = TOK // PARTS
SLAB = 512
FACTOR = D ** (-0.5)
N_COPIES = 136
N_LOADS = 16
f32, bf16 = jnp.float32, jnp.bfloat16

SCHEDULE = (
    ("f0", "n1", "N2", "N3", "C0", "Q0", "X0", "f1", "B0", "X1", "n2", "f2", "X2", "n3", "Z0", "f3")
    + ("Y0", "Z1", "X3", "b0", "U0", "Y1", "g0", "Z2", "U1", "V0", "b1", "Y2", "Z3", "g1")
    + ("U2", "V1", "Y3", "b2", "g2", "K0", "U3", "V2", "L0", "b3", "g3", "V3", "W0")
    + ("M0", "M1", "M2", "M3", "F0", "E0", "F1", "E1", "H0", "F2", "E2", "F3", "E3")
)


def kernel(
    tokens,
    gain_in,
    weight_in,
    cot_in,
    frag_in,
    global_in,
    moment_in,
    key_out,
    input_grad,
    weight_new,
    mixed,
    moment_new,
    global_new,
    tok,
    gain,
    weight,
    frag,
    glob,
    moment,
    cot,
    nin,
    nout,
    n_relay_buf,
    b_relay_buf,
    inv_s,
    bout,
    bin_,
    kp,
    kp1,
    kx,
    ksend,
    kc,
    xr,
    s1,
    s1_sent,
    zr,
    s2,
    yr,
    gx,
    send_sem,
    recv_sem,
    load_sem,
    near_sem,
    far_sem,
):
    r = lax.axis_index("replica")
    f = lax.axis_index("fsdp")
    x, yh, z = r // (NH * NZ), (r // NZ) % NH, r % NZ
    yl, core = f // 2, f % 2

    def fsdp_peer(q):
        a = 1 - yl if q & 2 else yl
        b = 1 - core if q & 1 else core
        return a * 2 + b

    def x_peer(d):
        return (((x + d) % NX) * NH + yh) * NZ + z, f

    def z_peer(d):
        return (x * NH + yh) * NZ + (z + d) % NZ, f

    y_peer = ((x * NH + (1 - yh)) * NZ + z, f)
    f_peer = {q: (r, fsdp_peer(q)) for q in (1, 2, 3)}

    loads = []

    def load(src, dst):
        copy = pltpu.make_async_copy(src, dst, load_sem.at[len(loads)])
        copy.start()
        loads.append(copy)
        return copy

    def block_cols(q):
        return pl.ds(pl.multiple_of((fsdp_peer(q) if q else f) * COLS, COLS), COLS)

    load_tok = [load(tokens.at[:, block_cols(q)], tok.at[q]) for q in range(NF)]
    load_gain = [load(gain_in.at[:, block_cols(q)], gain.at[q]) for q in range(NF)]
    load_cot = load(cot_in, cot.at[0])
    load_weight = load(weight_in.at[0], weight)
    load_frag = load(frag_in.at[0], frag)
    load_outer = [load(global_in.at[0], glob), load(moment_in.at[0], moment)]

    barrier = pltpu.get_barrier_semaphore()

    def tell(sem, device):
        pl.semaphore_signal(sem, 1, device_id=device, device_id_type=MESH)

    def fsdp_at(device, f):
        return device[0], f

    x_peers = [x_peer(d) for d in range(1, NX)]
    far_peers = [z_peer(d) for d in range(1, NZ)] + [y_peer]
    for peer in far_peers:
        tell(barrier, fsdp_at(peer, 3))

    @pl.when(core == 0)
    def _():
        tell(barrier, f_peer[2])
        for peer in x_peers:
            tell(barrier, peer)
        tell(barrier, (r, 1))

    @pl.when(f == 1)
    def _():
        for peer in x_peers:
            tell(barrier, peer)

    @pl.when(f == 3)
    def _():
        for peer in [(r, f)] + x_peers:
            tell(barrier, fsdp_at(peer, 1))

    def enter_near():
        @pl.when(core == 0)
        def _():
            pl.semaphore_wait(barrier, NX)

        @pl.when(f == 1)
        def _():
            pl.semaphore_wait(barrier, 2 * NX + 1)
            tell(near_sem, (r, 0))
            tell(near_sem, (r, 3))

        @pl.when(f == 3)
        def _():
            pl.semaphore_wait(near_sem, 1)
            tell(near_sem, (r, 2))

    def enter_chip():
        @pl.when(core == 0)
        def _():
            pl.semaphore_wait(near_sem, 1)

    def hear_far():
        @pl.when(f == 3)
        def _():
            pl.semaphore_wait(barrier, NF * len(far_peers))
            for other in range(3):
                tell(far_sem, (r, other))

    def enter_far():
        @pl.when(f != 3)
        def _():
            pl.semaphore_wait(far_sem, 1)

    copies = []

    def remote(src, dst, device):
        i = len(copies)
        copy = pltpu.make_async_remote_copy(
            src, dst, send_sem.at[i], recv_sem.at[i], device_id=device, device_id_type=MESH
        )
        copy.start()
        copies.append(copy)
        return copy

    def rows_of(c):
        return pl.ds(c * PR, PR)

    def fold(v):
        return v[:, :128] + v[:, 128:256] + v[:, 256:384] + v[:, 384:]

    def normalise(c):
        rows = rows_of(c)

        def square(q, acc):
            for s in range(COLS // SLAB):
                v = tok[q, rows, pl.ds(s * SLAB, SLAB)].astype(f32)
                acc = acc + fold(v * v)
            return acc

        acc = lax.fori_loop(0, NF, square, jnp.zeros((PR, 128), f32))
        inv = lax.rsqrt(jnp.sum(acc, axis=1, keepdims=True) * (1.0 / D) + norm_eps)
        inv_s[rows, :] = jnp.broadcast_to(inv, (PR, 128))

        def scale(q, dst):
            for s in range(COLS // SLAB):
                lanes = pl.ds(s * SLAB, SLAB)
                v = tok[q, rows, lanes].astype(f32)
                dst[q, rows, lanes] = (v * inv * gain[q, :, lanes]).astype(bf16)

        scale(0, nin)

        def others(q, _):
            scale(q, nout)
            return 0

        lax.fori_loop(1, NF, others, 0)

    def send_block(out, into, relay, c, q):
        rows = rows_of(c)
        if q == 3:
            return remote(out.at[3, rows], relay.at[rows], f_peer[1])
        return remote(out.at[q, rows], into.at[q, rows], f_peer[q])

    def pass_on(into, relay, c, copy):
        rows = rows_of(c)
        copy.wait_recv()
        return remote(relay.at[rows], into.at[3, rows], f_peer[2])

    def back_products():
        left = cot[...].reshape(NF * TOK, KV)

        def tile(t, _):
            rows = pl.ds(pl.multiple_of(t * 256, 256), 256)
            res = lax.dot_general(
                left, weight[rows, :], (((1,), (1,)), ((), ())), preferred_element_type=f32
            )
            res = (FACTOR * res).astype(bf16)
            bin_[0, :, rows] = res[:TOK]
            for q in range(1, NF):
                bout[q, :, rows] = res[q * TOK : (q + 1) * TOK]
            return 0

        lax.fori_loop(0, COLS // 256, tile, 0)

    def key_products():
        left = nin[...].reshape(NF * TOK, COLS)
        for n in range(2):
            lanes = pl.ds(n * 256, 256)
            res = jnp.dot(left, weight[:, lanes], preferred_element_type=f32)
            for q in range(NF):
                kp[q, :, lanes] = res[q * TOK : (q + 1) * TOK]

    def weight_products():
        right = cot[...].reshape(NF * TOK, KV)

        def tile(t, _):
            rows = pl.ds(pl.multiple_of(t * 256, 256), 256)
            left = nin[:, :, rows].reshape(NF * TOK, 256)
            res = lax.dot_general(
                left, right, (((0,), (0,)), ((), ())), preferred_element_type=f32
            )
            weight_new[0, rows, :] = (
                weight[rows, :].astype(f32) - inner_rate * (FACTOR * res)
            ).astype(bf16)
            return 0

        lax.fori_loop(0, COLS // 256, tile, 0)

    def finish_tokens(c):
        rows = rows_of(c)
        inv = inv_s[rows, :][:, :1]

        def project(q, acc):
            for s in range(COLS // SLAB):
                lanes = pl.ds(s * SLAB, SLAB)
                scaled = tok[q, rows, lanes].astype(f32) * inv
                gain_back = gain[q, :, lanes] * bin_[q, rows, lanes].astype(f32)
                acc = acc + fold(scaled * gain_back)
            return acc

        acc = lax.fori_loop(0, NF, project, jnp.zeros((PR, 128), f32))
        mean = jnp.sum(acc, axis=1, keepdims=True) * (1.0 / D)
        for q in range(NF):
            owner = fsdp_peer(q) if q else f
            for s in range(COLS // SLAB):
                lanes = pl.ds(s * SLAB, SLAB)
                scaled = tok[q, rows, lanes].astype(f32) * inv
                gain_back = gain[q, :, lanes] * bin_[q, rows, lanes].astype(f32)
                out = pl.ds(pl.multiple_of(owner * COLS + s * SLAB, SLAB), SLAB)
                input_grad[rows, out] = (inv * (gain_back - scaled * mean)).astype(bf16)

    def x_scatter(k):
        return [
            remote(
                frag_in.at[
                    0,
                    pl.ds(pl.multiple_of(((x + d) % NX) * XB, XB), XB),
                    pl.ds(k * KC, KC),
                ],
                xr.at[k, d - 1],
                x_peer(d),
            )
            for d in range(1, NX)
        ]

    def x_sum(k):
        lanes = pl.ds(k * KC, KC)
        for h in range(NH):
            base = ((yh + h) % NH) * (NZ * SHARE)

            def one(zi, _):
                at = base + zi * SHARE
                own = pl.ds(pl.multiple_of(x * XB + at, SHARE), SHARE)
                rows = pl.ds(pl.multiple_of(at, SHARE), SHARE)
                total = frag[own, lanes].astype(f32)
                for d in range(NX - 1):
                    total = total + xr[k, d, rows, :].astype(f32)
                s1[k, zi, h] = total
                s1_sent[k, zi, h] = total.astype(bf16)
                return 0

            lax.fori_loop(0, NZ, one, 0)

    def z_scatter(k):
        return [
            remote(s1_sent.at[k, (z + d) % NZ], zr.at[k, d - 1], z_peer(d)) for d in range(1, NZ)
        ]

    def z_sum(k):
        total = s1[k, z]
        for d in range(NZ - 1):
            total = total + zr[k, d].astype(f32)
        s2[k] = total

    def y_scatter(k):
        return remote(s2.at[k, 1], yr.at[k], y_peer)

    def update(k):
        lanes = pl.ds(k * KC, KC)
        mean = (s2[k, 0] + yr[k]) * (1.0 / REPLICAS)
        g = glob[:, lanes]
        outer_grad = g - mean
        m = momentum_decay * moment[:, lanes] + outer_grad
        g = g - outer_rate * (outer_grad + momentum_decay * m)
        moment_new[0, :, lanes] = m
        global_new[0, :, lanes] = g
        gx[0, k, 0, 0] = g.astype(bf16)

    def y_gather(k):
        return remote(gx.at[0, k, 0, 0], gx.at[0, k, 0, 1], y_peer)

    def z_gather(k):
        return [remote(gx.at[0, k, 0], gx.at[0, k, d], z_peer(d)) for d in range(1, NZ)]

    def x_gather(k):
        return [remote(gx.at[0, k], gx.at[e, k], x_peer(e)) for e in range(1, NX)]

    def mix(k, e):
        lanes = pl.ds(k * KC, KC)
        xi = (x + NX - e) % NX
        for h in range(NH):
            base = xi * XB + ((yh + h) % NH) * (NZ * SHARE)

            def one(d, _):
                at = base + ((z + NZ - d) % NZ) * SHARE
                rows = pl.ds(pl.multiple_of(at, SHARE), SHARE)
                mixed[0, rows, lanes] = (
                    mix_keep * frag[rows, lanes].astype(f32)
                    + (1.0 - mix_keep) * gx[e, k, d, h].astype(f32)
                ).astype(bf16)
                return 0

            lax.fori_loop(0, NZ, one, 0)

    def arrive(group):
        for copy in group if isinstance(group, list) else [group]:
            copy.wait_recv()

    live = {}

    def normed(c):
        normalise(c)
        live["nr", c] = send_block(nout, nin, n_relay_buf, c, 3)
        live["nl", c] = send_block(nout, nin, n_relay_buf, c, 1)

    def y_normed(c):
        live["nc", c] = send_block(nout, nin, n_relay_buf, c, 2)

    def pass_normed(c):
        live["np", c] = pass_on(nin, n_relay_buf, c, live["nr", c])

    def cot_on(_):
        arrive(live["cot2", 0])
        live["cot3", 0] = remote(cot.at[2], cot.at[3], f_peer[1])

    def back(_):
        load_cot.wait()
        load_weight.wait()
        arrive([live["cot1", 0], live["cot3", 0]])
        back_products()
        for c in range(PARTS):
            live["br", c] = send_block(bout, bin_, b_relay_buf, c, 3)
            live["bl", c] = send_block(bout, bin_, b_relay_buf, c, 1)

    def y_back(c):
        live["bc", c] = send_block(bout, bin_, b_relay_buf, c, 2)

    def pass_back(c):
        live["bp", c] = pass_on(bin_, b_relay_buf, c, live["br", c])

    def on_x(k):
        arrive(live["x", k])
        if k == 0:
            load_frag.wait()
        x_sum(k)
        if k == 0:
            enter_far()
        live["z", k] = z_scatter(k)

    def on_z(k):
        arrive(live["z", k])
        z_sum(k)
        live["y", k] = y_scatter(k)

    def on_y(k):
        if k == 0:
            for copy in load_outer:
                copy.wait()
        arrive(live["y", k])
        update(k)
        live["yg", k] = y_gather(k)

    def on_yg(k):
        arrive(live["yg", k])
        live["zg", k] = z_gather(k)

    def on_zg(k):
        arrive(live["zg", k])
        live["xg", k] = x_gather(k)

    def on_xg(k):
        arrive(live["xg", k])
        for e in range(1, NX):
            mix(k, e)

    def keys(_):
        arrive([live[n, c] for n in ("nl", "nc", "np") for c in range(PARTS)])
        key_products()
        live["k3", 0] = remote(kp.at[3], kx, f_peer[1])
        live["k1", 0] = remote(kp.at[1], kp1, f_peer[1])

    def keys_on(_):
        arrive(live["k3", 0])
        ksend[...] = (FACTOR * (kp[2] + kx[...])).astype(bf16)
        live["k2", 0] = remote(ksend, kc, f_peer[2])

    def keys_out(_):
        arrive([live["k1", 0], live["k2", 0]])
        key_out[...] = (FACTOR * (kp[0] + kp1[...]) + kc[...].astype(f32)).astype(bf16)

    def tokens_out(c):
        arrive([live[n, c] for n in ("bl", "bc", "bp")])
        finish_tokens(c)

    steps = {
        "N": normed,
        "n": y_normed,
        "f": pass_normed,
        "C": cot_on,
        "Q": lambda _: hear_far(),
        "B": back,
        "b": y_back,
        "g": pass_back,
        "X": on_x,
        "Z": on_z,
        "Y": on_y,
        "U": on_yg,
        "V": on_zg,
        "E": on_xg,
        "K": keys,
        "L": keys_on,
        "H": keys_out,
        "W": lambda _: weight_products(),
        "M": lambda k: mix(k, 0),
        "F": tokens_out,
    }

    for copy in load_tok + load_gain:
        copy.wait()
    normalise(0)
    enter_near()
    live["cot2", 0] = remote(cot_in, cot.at[2], f_peer[2])
    live["x", 0] = x_scatter(0)
    y_normed(0)
    for k in range(1, K):
        live["x", k] = x_scatter(k)
    normalise(1)
    enter_chip()
    for c in range(2):
        live["nr", c] = send_block(nout, nin, n_relay_buf, c, 3)
        live["nl", c] = send_block(nout, nin, n_relay_buf, c, 1)
    live["cot1", 0] = remote(cot_in, cot.at[1], f_peer[1])
    for step in SCHEDULE:
        steps[step[0]](int(step[1:]))
    for copy in copies:
        copy.wait_send()


def write_out(*refs):
    sources, targets, sem = refs[:6], refs[6:12], refs[12]
    copies = [
        pltpu.make_async_copy(s, t, sem.at[i])
        for i, (s, t) in enumerate(zip(sources, targets, strict=True))
    ]
    for copy in copies:
        copy.start()
    for copy in copies:
        copy.wait()


def local(
    tokens, norm_gain, key_weight, key_cotangent, fragment_local, fragment_global, outer_moment
):
    hbm = pl.BlockSpec(memory_space=pltpu.HBM)
    vmem = pl.BlockSpec(memory_space=pltpu.VMEM)
    shapes = (
        jax.ShapeDtypeStruct((TOK, KV), bf16),
        jax.ShapeDtypeStruct((TOK, D), bf16),
        jax.ShapeDtypeStruct((1, COLS, KV), bf16),
        jax.ShapeDtypeStruct((1, COLS, KV), bf16),
        jax.ShapeDtypeStruct((1, SHARE, KV), f32),
        jax.ShapeDtypeStruct((1, SHARE, KV), f32),
    )
    results = pl.pallas_call(
        kernel,
        name="diloco_step",
        out_shape=shapes,
        in_specs=[hbm] * 7,
        out_specs=(vmem,) * 6,
        scratch_shapes=[
            pltpu.VMEM((NF, TOK, COLS), bf16),
            pltpu.VMEM((NF, 1, COLS), f32),
            pltpu.VMEM((COLS, KV), bf16),
            pltpu.VMEM((COLS, KV), bf16),
            pltpu.VMEM((SHARE, KV), f32),
            pltpu.VMEM((SHARE, KV), f32),
            pltpu.VMEM((NF, TOK, KV), bf16),
            pltpu.VMEM((NF, TOK, COLS), bf16),
            pltpu.VMEM((NF, TOK, COLS), bf16),
            pltpu.VMEM((TOK, COLS), bf16),
            pltpu.VMEM((TOK, COLS), bf16),
            pltpu.VMEM((TOK, 128), f32),
            pltpu.VMEM((NF, TOK, COLS), bf16),
            pltpu.VMEM((NF, TOK, COLS), bf16),
            pltpu.VMEM((NF, TOK, KV), f32),
            pltpu.VMEM((TOK, KV), f32),
            pltpu.VMEM((TOK, KV), f32),
            pltpu.VMEM((TOK, KV), bf16),
            pltpu.VMEM((TOK, KV), bf16),
            pltpu.VMEM((K, NX - 1, XB, KC), bf16),
            pltpu.VMEM((K, NZ, NH, SHARE, KC), f32),
            pltpu.VMEM((K, NZ, NH, SHARE, KC), bf16),
            pltpu.VMEM((K, NZ - 1, NH, SHARE, KC), bf16),
            pltpu.VMEM((K, NH, SHARE, KC), f32),
            pltpu.VMEM((K, SHARE, KC), f32),
            pltpu.VMEM((NX, K, NZ, NH, SHARE, KC), bf16),
            pltpu.SemaphoreType.DMA((N_COPIES,)),
            pltpu.SemaphoreType.DMA((N_COPIES,)),
            pltpu.SemaphoreType.DMA((N_LOADS,)),
            pltpu.SemaphoreType.REGULAR,
            pltpu.SemaphoreType.REGULAR,
        ],
        compiler_params=pltpu.CompilerParams(
            collective_id=0, has_side_effects=True, vmem_limit_bytes=36 << 20
        ),
    )(
        *(
            pltpu.with_memory_space_constraint(a, pltpu.HBM)
            for a in (
                tokens,
                norm_gain[None],
                key_weight,
                key_cotangent,
                fragment_local,
                fragment_global,
                outer_moment,
            )
        )
    )
    return pl.pallas_call(
        write_out,
        name="write_out",
        out_shape=shapes,
        in_specs=[vmem] * 6,
        out_specs=(hbm,) * 6,
        scratch_shapes=[pltpu.SemaphoreType.DMA((6,))],
        compiler_params=pltpu.CompilerParams(vmem_limit_bytes=1 << 20),
    )(*results)


def solution(mesh):
    return jax.shard_map(
        local,
        mesh=mesh,
        in_specs=(
            P(("replica", "fsdp"), None),
            P(),
            P("replica", "fsdp", None),
            P(("replica", "fsdp"), None),
            P("replica", "fsdp", None),
            P("fsdp", "replica", None),
            P("fsdp", "replica", None),
        ),
        out_specs=(
            P(("replica", "fsdp"), None),
            P(("replica", "fsdp"), None),
            P("replica", "fsdp", None),
            P("replica", "fsdp", None),
            P("fsdp", "replica", None),
            P("fsdp", "replica", None),
        ),
        check_vma=False,
    )
```

```python
import jax
import jax.numpy as jnp
from jax import lax
from jax.experimental import pallas as pl
from jax.experimental.pallas import tpu as pltpu
from jax.sharding import PartitionSpec as P

norm_eps = 1e-05
inner_rate = 1.0
outer_rate = 0.7
momentum_decay = 0.9
mix_keep = 0.5

MESH = pl.DeviceIdType.MESH
NX, NH, NZ, NF = 4, 2, 8, 4
REPLICAS = NX * NH * NZ
TOK, D, KV = 128, 8192, 512
COLS = D // NF
SHARE = COLS // REPLICAS
XB = COLS // NX
K = 4
KC = KV // K
PARTS = 4
PR = TOK // PARTS
SLAB = 512
FACTOR = D ** (-0.5)
N_COPIES = 136
N_LOADS = 16
f32, bf16 = jnp.float32, jnp.bfloat16

SCHEDULE = (
    ("f0", "n1", "N2", "N3", "C0", "Q0", "X0", "f1", "n2", "B0", "X1", "f2", "n3", "Z0", "f3", "X2")
    + ("Z1", "b0", "Y0", "X3", "g0", "Z2", "Y1", "b1", "V0", "Z3", "g1", "Y2")
    + ("b2", "V1", "Y3", "g2", "b3", "V2", "K0", "g3", "L0", "V3", "W0")
    + ("M0", "M1", "M2", "M3", "F0", "E0", "F1", "E1", "H0", "F2", "E2", "F3", "E3")
)


def kernel(
    tokens,
    gain_in,
    weight_in,
    cot_in,
    frag_in,
    global_in,
    moment_in,
    key_out,
    input_grad,
    weight_new,
    mixed,
    moment_new,
    global_new,
    tok,
    gain,
    weight,
    frag,
    glob,
    moment,
    cot,
    nin,
    nout,
    n_relay_buf,
    b_relay_buf,
    inv_s,
    bout,
    bin_,
    kp,
    kp1,
    kx,
    ksend,
    kc,
    xr,
    s1,
    s1_sent,
    zr,
    s2,
    yr,
    base,
    gx,
    send_sem,
    recv_sem,
    load_sem,
    near_sem,
    far_sem,
):
    r = lax.axis_index("replica")
    f = lax.axis_index("fsdp")
    x, yh, z = r // (NH * NZ), (r // NZ) % NH, r % NZ
    yl, core = f // 2, f % 2

    def fsdp_peer(q):
        a = 1 - yl if q & 2 else yl
        b = 1 - core if q & 1 else core
        return a * 2 + b

    def x_peer(d):
        return (((x + d) % NX) * NH + yh) * NZ + z, f

    def z_peer(d):
        return (x * NH + yh) * NZ + (z + d) % NZ, f

    y_peer = ((x * NH + (1 - yh)) * NZ + z, f)
    f_peer = {q: (r, fsdp_peer(q)) for q in (1, 2, 3)}

    loads = []

    def load(src, dst):
        copy = pltpu.make_async_copy(src, dst, load_sem.at[len(loads)])
        copy.start()
        loads.append(copy)
        return copy

    def block_cols(q):
        return pl.ds(pl.multiple_of((fsdp_peer(q) if q else f) * COLS, COLS), COLS)

    load_tok = [load(tokens.at[:, block_cols(q)], tok.at[q]) for q in range(NF)]
    load_gain = [load(gain_in.at[:, block_cols(q)], gain.at[q]) for q in range(NF)]
    load_cot = load(cot_in, cot.at[0])
    load_weight = load(weight_in.at[0], weight)
    load_frag = load(frag_in.at[0], frag)
    load_outer = [load(global_in.at[0], glob), load(moment_in.at[0], moment)]

    barrier = pltpu.get_barrier_semaphore()

    def tell(sem, device):
        pl.semaphore_signal(sem, 1, device_id=device, device_id_type=MESH)

    def fsdp_at(device, f):
        return device[0], f

    x_peers = [x_peer(d) for d in range(1, NX)]
    far_peers = [z_peer(d) for d in range(1, NZ)] + [y_peer]
    for peer in far_peers:
        tell(barrier, fsdp_at(peer, 3))

    @pl.when(core == 0)
    def _():
        tell(barrier, f_peer[2])
        for peer in x_peers:
            tell(barrier, peer)
        tell(barrier, (r, 1))

    @pl.when(f == 1)
    def _():
        for peer in x_peers:
            tell(barrier, peer)

    @pl.when(f == 3)
    def _():
        for peer in [(r, f)] + x_peers:
            tell(barrier, fsdp_at(peer, 1))

    def enter_near():
        @pl.when(core == 0)
        def _():
            pl.semaphore_wait(barrier, NX)

        @pl.when(f == 1)
        def _():
            pl.semaphore_wait(barrier, 2 * NX + 1)
            tell(near_sem, (r, 0))
            tell(near_sem, (r, 3))

        @pl.when(f == 3)
        def _():
            pl.semaphore_wait(near_sem, 1)
            tell(near_sem, (r, 2))

    def enter_chip():
        @pl.when(core == 0)
        def _():
            pl.semaphore_wait(near_sem, 1)

    def hear_far():
        @pl.when(f == 3)
        def _():
            pl.semaphore_wait(barrier, NF * len(far_peers))
            for other in range(3):
                tell(far_sem, (r, other))

    def enter_far():
        @pl.when(f != 3)
        def _():
            pl.semaphore_wait(far_sem, 1)

    copies = []

    def remote(src, dst, device):
        i = len(copies)
        copy = pltpu.make_async_remote_copy(
            src, dst, send_sem.at[i], recv_sem.at[i], device_id=device, device_id_type=MESH
        )
        copy.start()
        copies.append(copy)
        return copy

    def rows_of(c):
        return pl.ds(c * PR, PR)

    def fold(v):
        return v[:, :128] + v[:, 128:256] + v[:, 256:384] + v[:, 384:]

    def normalise(c):
        rows = rows_of(c)

        def square(q, acc):
            for s in range(COLS // SLAB):
                v = tok[q, rows, pl.ds(s * SLAB, SLAB)].astype(f32)
                acc = acc + fold(v * v)
            return acc

        acc = lax.fori_loop(0, NF, square, jnp.zeros((PR, 128), f32))
        inv = lax.rsqrt(jnp.sum(acc, axis=1, keepdims=True) * (1.0 / D) + norm_eps)
        inv_s[rows, :] = jnp.broadcast_to(inv, (PR, 128))

        def scale(q, dst):
            for s in range(COLS // SLAB):
                lanes = pl.ds(s * SLAB, SLAB)
                v = tok[q, rows, lanes].astype(f32)
                dst[q, rows, lanes] = (v * inv * gain[q, :, lanes]).astype(bf16)

        scale(0, nin)

        def others(q, _):
            scale(q, nout)
            return 0

        lax.fori_loop(1, NF, others, 0)

    def send_block(out, into, relay, c, q):
        rows = rows_of(c)
        if q == 3:
            return remote(out.at[3, rows], relay.at[rows], f_peer[1])
        return remote(out.at[q, rows], into.at[q, rows], f_peer[q])

    def pass_on(into, relay, c, copy):
        rows = rows_of(c)
        copy.wait_recv()
        return remote(relay.at[rows], into.at[3, rows], f_peer[2])

    def back_products():
        left = cot[...].reshape(NF * TOK, KV)

        def tile(t, _):
            rows = pl.ds(pl.multiple_of(t * 256, 256), 256)
            res = lax.dot_general(
                left, weight[rows, :], (((1,), (1,)), ((), ())), preferred_element_type=f32
            )
            res = (FACTOR * res).astype(bf16)
            bin_[0, :, rows] = res[:TOK]
            for q in range(1, NF):
                bout[q, :, rows] = res[q * TOK : (q + 1) * TOK]
            return 0

        lax.fori_loop(0, COLS // 256, tile, 0)

    def key_products():
        left = nin[...].reshape(NF * TOK, COLS)
        for n in range(2):
            lanes = pl.ds(n * 256, 256)
            res = jnp.dot(left, weight[:, lanes], preferred_element_type=f32)
            for q in range(NF):
                kp[q, :, lanes] = res[q * TOK : (q + 1) * TOK]

    def weight_products():
        right = cot[...].reshape(NF * TOK, KV)

        def tile(t, _):
            rows = pl.ds(pl.multiple_of(t * 256, 256), 256)
            left = nin[:, :, rows].reshape(NF * TOK, 256)
            res = lax.dot_general(
                left, right, (((0,), (0,)), ((), ())), preferred_element_type=f32
            )
            weight_new[0, rows, :] = (
                weight[rows, :].astype(f32) - inner_rate * (FACTOR * res)
            ).astype(bf16)
            return 0

        lax.fori_loop(0, COLS // 256, tile, 0)

    def finish_tokens(c):
        rows = rows_of(c)
        inv = inv_s[rows, :][:, :1]

        def project(q, acc):
            for s in range(COLS // SLAB):
                lanes = pl.ds(s * SLAB, SLAB)
                scaled = tok[q, rows, lanes].astype(f32) * inv
                gain_back = gain[q, :, lanes] * bin_[q, rows, lanes].astype(f32)
                acc = acc + fold(scaled * gain_back)
            return acc

        acc = lax.fori_loop(0, NF, project, jnp.zeros((PR, 128), f32))
        mean = jnp.sum(acc, axis=1, keepdims=True) * (1.0 / D)
        for q in range(NF):
            owner = fsdp_peer(q) if q else f
            for s in range(COLS // SLAB):
                lanes = pl.ds(s * SLAB, SLAB)
                scaled = tok[q, rows, lanes].astype(f32) * inv
                gain_back = gain[q, :, lanes] * bin_[q, rows, lanes].astype(f32)
                out = pl.ds(pl.multiple_of(owner * COLS + s * SLAB, SLAB), SLAB)
                input_grad[rows, out] = (inv * (gain_back - scaled * mean)).astype(bf16)

    def x_scatter(k):
        return [
            remote(
                frag_in.at[
                    0,
                    pl.ds(pl.multiple_of(((x + d) % NX) * XB, XB), XB),
                    pl.ds(k * KC, KC),
                ],
                xr.at[k, d - 1],
                x_peer(d),
            )
            for d in range(1, NX)
        ]

    def x_sum(k):
        lanes = pl.ds(k * KC, KC)
        for h in range(NH):
            first = ((yh + h) % NH) * (NZ * SHARE)

            def one(zi, _):
                at = first + zi * SHARE
                own = pl.ds(pl.multiple_of(x * XB + at, SHARE), SHARE)
                rows = pl.ds(pl.multiple_of(at, SHARE), SHARE)
                total = frag[own, lanes].astype(f32)
                for d in range(NX - 1):
                    total = total + xr[k, d, rows, :].astype(f32)
                s1[k, zi, h] = total
                s1_sent[k, zi, h] = total.astype(bf16)
                return 0

            lax.fori_loop(0, NZ, one, 0)

    def z_scatter(k):
        return [
            remote(s1_sent.at[k, (z + d) % NZ], zr.at[k, d - 1], z_peer(d)) for d in range(1, NZ)
        ]

    def z_sum(k):
        total = s1[k, z]
        for d in range(NZ - 1):
            total = total + zr[k, d].astype(f32)
        s2[k] = total.astype(bf16)

    pull = outer_rate * (1.0 + momentum_decay)

    def outer_base():
        g = glob[...]
        base[0] = g - (pull * g + (outer_rate * momentum_decay**2) * moment[...])
        return remote(base.at[0], base.at[1], y_peer)

    def y_swap(k):
        return remote(s2.at[k], yr.at[k], y_peer)

    def update(k):
        lanes = pl.ds(k * KC, KC)
        for h in range(NH):
            mean = (s2[k, h].astype(f32) + yr[k, 1 - h].astype(f32)) * (1.0 / REPLICAS)
            gx[0, k, 0, h] = (base[h, :, lanes] + pull * mean).astype(bf16)
            if h == 0:
                g = glob[:, lanes]
                outer_grad = g - mean
                m = momentum_decay * moment[:, lanes] + outer_grad
                moment_new[0, :, lanes] = m
                global_new[0, :, lanes] = g - outer_rate * (outer_grad + momentum_decay * m)

    def z_gather(k):
        return [remote(gx.at[0, k, 0], gx.at[0, k, d], z_peer(d)) for d in range(1, NZ)]

    def x_gather(k):
        return [remote(gx.at[0, k], gx.at[e, k], x_peer(e)) for e in range(1, NX)]

    def mix(k, e):
        lanes = pl.ds(k * KC, KC)
        xi = (x + NX - e) % NX
        for h in range(NH):
            first = xi * XB + ((yh + h) % NH) * (NZ * SHARE)

            def one(d, _):
                at = first + ((z + NZ - d) % NZ) * SHARE
                rows = pl.ds(pl.multiple_of(at, SHARE), SHARE)
                mixed[0, rows, lanes] = (
                    mix_keep * frag[rows, lanes].astype(f32)
                    + (1.0 - mix_keep) * gx[e, k, d, h].astype(f32)
                ).astype(bf16)
                return 0

            lax.fori_loop(0, NZ, one, 0)

    def arrive(group):
        for copy in group if isinstance(group, list) else [group]:
            copy.wait_recv()

    live = {}

    def normed(c):
        normalise(c)
        live["nr", c] = send_block(nout, nin, n_relay_buf, c, 3)
        live["nl", c] = send_block(nout, nin, n_relay_buf, c, 1)

    def y_normed(c):
        live["nc", c] = send_block(nout, nin, n_relay_buf, c, 2)

    def pass_normed(c):
        live["np", c] = pass_on(nin, n_relay_buf, c, live["nr", c])

    def cot_on(_):
        arrive(live["cot2", 0])
        live["cot3", 0] = remote(cot.at[2], cot.at[3], f_peer[1])

    def back(_):
        load_cot.wait()
        load_weight.wait()
        arrive([live["cot1", 0], live["cot3", 0]])
        back_products()
        for c in range(PARTS):
            live["br", c] = send_block(bout, bin_, b_relay_buf, c, 3)
            live["bl", c] = send_block(bout, bin_, b_relay_buf, c, 1)

    def y_back(c):
        live["bc", c] = send_block(bout, bin_, b_relay_buf, c, 2)

    def pass_back(c):
        live["bp", c] = pass_on(bin_, b_relay_buf, c, live["br", c])

    def on_x(k):
        arrive(live["x", k])
        if k == 0:
            load_frag.wait()
        x_sum(k)
        if k == 0:
            enter_far()
            for copy in load_outer:
                copy.wait()
            live["base", 0] = outer_base()
        live["z", k] = z_scatter(k)

    def on_z(k):
        arrive(live["z", k])
        z_sum(k)
        live["y", k] = y_swap(k)

    def on_y(k):
        if k == 0:
            arrive(live["base", 0])
        arrive(live["y", k])
        update(k)
        live["zg", k] = z_gather(k)

    def on_zg(k):
        arrive(live["zg", k])
        live["xg", k] = x_gather(k)

    def on_xg(k):
        arrive(live["xg", k])
        for e in range(1, NX):
            mix(k, e)

    def keys(_):
        arrive([live[n, c] for n in ("nl", "nc", "np") for c in range(PARTS)])
        key_products()
        live["k3", 0] = remote(kp.at[3], kx, f_peer[1])
        live["k1", 0] = remote(kp.at[1], kp1, f_peer[1])

    def keys_on(_):
        arrive(live["k3", 0])
        ksend[...] = (FACTOR * (kp[2] + kx[...])).astype(bf16)
        live["k2", 0] = remote(ksend, kc, f_peer[2])

    def keys_out(_):
        arrive([live["k1", 0], live["k2", 0]])
        key_out[...] = (FACTOR * (kp[0] + kp1[...]) + kc[...].astype(f32)).astype(bf16)

    def tokens_out(c):
        arrive([live[n, c] for n in ("bl", "bc", "bp")])
        finish_tokens(c)

    steps = {
        "N": normed,
        "n": y_normed,
        "f": pass_normed,
        "C": cot_on,
        "Q": lambda _: hear_far(),
        "B": back,
        "b": y_back,
        "g": pass_back,
        "X": on_x,
        "Z": on_z,
        "Y": on_y,
        "V": on_zg,
        "E": on_xg,
        "K": keys,
        "L": keys_on,
        "H": keys_out,
        "W": lambda _: weight_products(),
        "M": lambda k: mix(k, 0),
        "F": tokens_out,
    }

    enter_near()
    live["cot2", 0] = remote(cot_in, cot.at[2], f_peer[2])
    for k in range(K):
        live["x", k] = x_scatter(k)
    for copy in load_tok + load_gain:
        copy.wait()
    normalise(0)
    y_normed(0)
    normalise(1)
    enter_chip()
    for c in range(2):
        live["nr", c] = send_block(nout, nin, n_relay_buf, c, 3)
        live["nl", c] = send_block(nout, nin, n_relay_buf, c, 1)
    live["cot1", 0] = remote(cot_in, cot.at[1], f_peer[1])
    for step in SCHEDULE:
        steps[step[0]](int(step[1:]))
    for copy in copies:
        copy.wait_send()


def write_out(*refs):
    sources, targets, sem = refs[:6], refs[6:12], refs[12]
    copies = [
        pltpu.make_async_copy(s, t, sem.at[i])
        for i, (s, t) in enumerate(zip(sources, targets, strict=True))
    ]
    for copy in copies:
        copy.start()
    for copy in copies:
        copy.wait()


def local(
    tokens, norm_gain, key_weight, key_cotangent, fragment_local, fragment_global, outer_moment
):
    hbm = pl.BlockSpec(memory_space=pltpu.HBM)
    vmem = pl.BlockSpec(memory_space=pltpu.VMEM)
    shapes = (
        jax.ShapeDtypeStruct((TOK, KV), bf16),
        jax.ShapeDtypeStruct((TOK, D), bf16),
        jax.ShapeDtypeStruct((1, COLS, KV), bf16),
        jax.ShapeDtypeStruct((1, COLS, KV), bf16),
        jax.ShapeDtypeStruct((1, SHARE, KV), f32),
        jax.ShapeDtypeStruct((1, SHARE, KV), f32),
    )
    results = pl.pallas_call(
        kernel,
        name="diloco_step",
        out_shape=shapes,
        in_specs=[hbm] * 7,
        out_specs=(vmem,) * 6,
        scratch_shapes=[
            pltpu.VMEM((NF, TOK, COLS), bf16),
            pltpu.VMEM((NF, 1, COLS), f32),
            pltpu.VMEM((COLS, KV), bf16),
            pltpu.VMEM((COLS, KV), bf16),
            pltpu.VMEM((SHARE, KV), f32),
            pltpu.VMEM((SHARE, KV), f32),
            pltpu.VMEM((NF, TOK, KV), bf16),
            pltpu.VMEM((NF, TOK, COLS), bf16),
            pltpu.VMEM((NF, TOK, COLS), bf16),
            pltpu.VMEM((TOK, COLS), bf16),
            pltpu.VMEM((TOK, COLS), bf16),
            pltpu.VMEM((TOK, 128), f32),
            pltpu.VMEM((NF, TOK, COLS), bf16),
            pltpu.VMEM((NF, TOK, COLS), bf16),
            pltpu.VMEM((NF, TOK, KV), f32),
            pltpu.VMEM((TOK, KV), f32),
            pltpu.VMEM((TOK, KV), f32),
            pltpu.VMEM((TOK, KV), bf16),
            pltpu.VMEM((TOK, KV), bf16),
            pltpu.VMEM((K, NX - 1, XB, KC), bf16),
            pltpu.VMEM((K, NZ, NH, SHARE, KC), f32),
            pltpu.VMEM((K, NZ, NH, SHARE, KC), bf16),
            pltpu.VMEM((K, NZ - 1, NH, SHARE, KC), bf16),
            pltpu.VMEM((K, NH, SHARE, KC), bf16),
            pltpu.VMEM((K, NH, SHARE, KC), bf16),
            pltpu.VMEM((NH, SHARE, KV), f32),
            pltpu.VMEM((NX, K, NZ, NH, SHARE, KC), bf16),
            pltpu.SemaphoreType.DMA((N_COPIES,)),
            pltpu.SemaphoreType.DMA((N_COPIES,)),
            pltpu.SemaphoreType.DMA((N_LOADS,)),
            pltpu.SemaphoreType.REGULAR,
            pltpu.SemaphoreType.REGULAR,
        ],
        compiler_params=pltpu.CompilerParams(
            collective_id=0, has_side_effects=True, vmem_limit_bytes=36 << 20
        ),
    )(
        *(
            pltpu.with_memory_space_constraint(a, pltpu.HBM)
            for a in (
                tokens,
                norm_gain[None],
                key_weight,
                key_cotangent,
                fragment_local,
                fragment_global,
                outer_moment,
            )
        )
    )
    return pl.pallas_call(
        write_out,
        name="write_out",
        out_shape=shapes,
        in_specs=[vmem] * 6,
        out_specs=(hbm,) * 6,
        scratch_shapes=[pltpu.SemaphoreType.DMA((6,))],
        compiler_params=pltpu.CompilerParams(vmem_limit_bytes=1 << 20),
    )(*results)


def solution(mesh):
    return jax.shard_map(
        local,
        mesh=mesh,
        in_specs=(
            P(("replica", "fsdp"), None),
            P(),
            P("replica", "fsdp", None),
            P(("replica", "fsdp"), None),
            P("replica", "fsdp", None),
            P("fsdp", "replica", None),
            P("fsdp", "replica", None),
        ),
        out_specs=(
            P(("replica", "fsdp"), None),
            P(("replica", "fsdp"), None),
            P("replica", "fsdp", None),
            P("replica", "fsdp", None),
            P("fsdp", "replica", None),
            P("fsdp", "replica", None),
        ),
        check_vma=False,
    )
```

```python
import jax
import jax.numpy as jnp
from jax import lax
from jax.experimental import pallas as pl
from jax.experimental.pallas import tpu as pltpu
from jax.sharding import PartitionSpec as P

norm_eps = 1e-05
inner_rate = 1.0
outer_rate = 0.7
momentum_decay = 0.9
mix_keep = 0.5

MESH = pl.DeviceIdType.MESH
NX, NH, NZ, NF = 4, 2, 8, 4
REPLICAS = NX * NH * NZ
TOK, D, KV = 128, 8192, 512
COLS = D // NF
SHARE = COLS // REPLICAS
XB = COLS // NX
K = 4
KC = KV // K
PARTS = 4
PR = TOK // PARTS
SLAB = 512
FACTOR = D ** (-0.5)
N_COPIES = 136
N_LOADS = 16
f32, bf16 = jnp.float32, jnp.bfloat16

SCHEDULE = (
    ("f0", "n1", "N2", "N3", "C0", "Q0", "X0", "f1", "n2", "B0", "X1", "f2", "n3", "Z0", "f3", "X2")
    + ("Z1", "b0", "Y0", "X3", "g0", "Z2", "Y1", "b1", "V0", "Z3", "g1", "Y2")
    + ("b2", "V1", "Y3", "g2", "b3", "V2", "K0", "g3", "V3", "L0", "W0")
    + ("M0", "M1", "M2", "M3", "F0", "E0", "F1", "E1", "H0", "F2", "E2", "F3", "E3")
)


def kernel(
    tokens,
    gain_in,
    weight_in,
    cot_in,
    frag_in,
    global_in,
    moment_in,
    key_out,
    input_grad,
    weight_new,
    mixed,
    moment_new,
    global_new,
    tok,
    gain,
    weight,
    frag,
    glob,
    moment,
    cot,
    nin,
    nout,
    n_relay_buf,
    b_relay_buf,
    inv_s,
    bout,
    bin_,
    kp,
    kp1,
    kx,
    ksend,
    kc,
    xr,
    s1,
    s1_sent,
    zr,
    s2,
    yr,
    base,
    gx,
    send_sem,
    recv_sem,
    load_sem,
    near_sem,
    far_sem,
):
    r = lax.axis_index("replica")
    f = lax.axis_index("fsdp")
    x, yh, z = r // (NH * NZ), (r // NZ) % NH, r % NZ
    yl, core = f // 2, f % 2

    def fsdp_peer(q):
        a = 1 - yl if q & 2 else yl
        b = 1 - core if q & 1 else core
        return a * 2 + b

    def x_peer(d):
        return (((x + d) % NX) * NH + yh) * NZ + z, f

    def z_peer(d):
        return (x * NH + yh) * NZ + (z + d) % NZ, f

    y_peer = ((x * NH + (1 - yh)) * NZ + z, f)
    f_peer = {q: (r, fsdp_peer(q)) for q in (1, 2, 3)}

    loads = []

    def load(src, dst):
        copy = pltpu.make_async_copy(src, dst, load_sem.at[len(loads)])
        copy.start()
        loads.append(copy)
        return copy

    def block_cols(q):
        return pl.ds(pl.multiple_of((fsdp_peer(q) if q else f) * COLS, COLS), COLS)

    load_tok = [load(tokens.at[:, block_cols(q)], tok.at[q]) for q in range(NF)]
    load_gain = [load(gain_in.at[:, block_cols(q)], gain.at[q]) for q in range(NF)]
    load_cot = load(cot_in, cot.at[0])
    load_weight = load(weight_in.at[0], weight)
    load_frag = load(frag_in.at[0], frag)
    load_outer = [load(global_in.at[0], glob), load(moment_in.at[0], moment)]

    barrier = pltpu.get_barrier_semaphore()

    def tell(sem, device):
        pl.semaphore_signal(sem, 1, device_id=device, device_id_type=MESH)

    def fsdp_at(device, f):
        return device[0], f

    x_peers = [x_peer(d) for d in range(1, NX)]
    far_peers = [z_peer(d) for d in range(1, NZ)] + [y_peer]
    for peer in far_peers:
        tell(barrier, fsdp_at(peer, 3))

    @pl.when(core == 0)
    def _():
        tell(barrier, f_peer[2])
        for peer in x_peers:
            tell(barrier, peer)
        tell(barrier, (r, 1))

    @pl.when(f == 1)
    def _():
        for peer in x_peers:
            tell(barrier, peer)

    @pl.when(f == 3)
    def _():
        for peer in [(r, f)] + x_peers:
            tell(barrier, fsdp_at(peer, 1))

    def enter_near():
        @pl.when(core == 0)
        def _():
            pl.semaphore_wait(barrier, NX)

        @pl.when(f == 1)
        def _():
            pl.semaphore_wait(barrier, 2 * NX + 1)
            tell(near_sem, (r, 0))
            tell(near_sem, (r, 3))

        @pl.when(f == 3)
        def _():
            pl.semaphore_wait(near_sem, 1)
            tell(near_sem, (r, 2))

    def enter_chip():
        @pl.when(core == 0)
        def _():
            pl.semaphore_wait(near_sem, 1)

    def hear_far():
        @pl.when(f == 3)
        def _():
            pl.semaphore_wait(barrier, NF * len(far_peers))
            for other in range(3):
                tell(far_sem, (r, other))

    def enter_far():
        @pl.when(f != 3)
        def _():
            pl.semaphore_wait(far_sem, 1)

    copies = []

    def remote(src, dst, device):
        i = len(copies)
        copy = pltpu.make_async_remote_copy(
            src, dst, send_sem.at[i], recv_sem.at[i], device_id=device, device_id_type=MESH
        )
        copy.start()
        copies.append(copy)
        return copy

    def rows_of(c):
        return pl.ds(c * PR, PR)

    def fold(v):
        return v[:, :128] + v[:, 128:256] + v[:, 256:384] + v[:, 384:]

    def normalise(c):
        rows = rows_of(c)

        def square(q, acc):
            for s in range(COLS // SLAB):
                v = tok[q, rows, pl.ds(s * SLAB, SLAB)].astype(f32)
                acc = acc + fold(v * v)
            return acc

        acc = lax.fori_loop(0, NF, square, jnp.zeros((PR, 128), f32))
        inv = lax.rsqrt(jnp.sum(acc, axis=1, keepdims=True) * (1.0 / D) + norm_eps)
        inv_s[rows, :] = jnp.broadcast_to(inv, (PR, 128))

        def scale(q, dst):
            for s in range(COLS // SLAB):
                lanes = pl.ds(s * SLAB, SLAB)
                v = tok[q, rows, lanes].astype(f32)
                dst[q, rows, lanes] = (v * inv * gain[q, :, lanes]).astype(bf16)

        scale(0, nin)

        def others(q, _):
            scale(q, nout)
            return 0

        lax.fori_loop(1, NF, others, 0)

    def send_block(out, into, relay, c, q):
        rows = rows_of(c)
        if q == 3:
            return remote(out.at[3, rows], relay.at[rows], f_peer[1])
        return remote(out.at[q, rows], into.at[q, rows], f_peer[q])

    def pass_on(into, relay, c, copy):
        rows = rows_of(c)
        copy.wait_recv()
        return remote(relay.at[rows], into.at[3, rows], f_peer[2])

    def back_products():
        left = cot[...].reshape(NF * TOK, KV)

        def tile(t, _):
            rows = pl.ds(pl.multiple_of(t * 256, 256), 256)
            res = lax.dot_general(
                left, weight[rows, :], (((1,), (1,)), ((), ())), preferred_element_type=f32
            )
            res = (FACTOR * res).astype(bf16)
            bin_[0, :, rows] = res[:TOK]
            for q in range(1, NF):
                bout[q, :, rows] = res[q * TOK : (q + 1) * TOK]
            return 0

        lax.fori_loop(0, COLS // 256, tile, 0)

    def key_products():
        left = nin[...].reshape(NF * TOK, COLS)
        for n in range(2):
            lanes = pl.ds(n * 256, 256)
            res = jnp.dot(left, weight[:, lanes], preferred_element_type=f32)
            for q in range(NF):
                kp[q, :, lanes] = res[q * TOK : (q + 1) * TOK]

    def weight_products():
        right = cot[...].reshape(NF * TOK, KV)

        def tile(t, _):
            rows = pl.ds(pl.multiple_of(t * 256, 256), 256)
            left = nin[:, :, rows].reshape(NF * TOK, 256)
            res = lax.dot_general(
                left, right, (((0,), (0,)), ((), ())), preferred_element_type=f32
            )
            weight_new[0, rows, :] = (
                weight[rows, :].astype(f32) - inner_rate * (FACTOR * res)
            ).astype(bf16)
            return 0

        lax.fori_loop(0, COLS // 256, tile, 0)

    def finish_tokens(c):
        rows = rows_of(c)
        inv = inv_s[rows, :][:, :1]

        def project(q, acc):
            for s in range(COLS // SLAB):
                lanes = pl.ds(s * SLAB, SLAB)
                scaled = tok[q, rows, lanes].astype(f32) * inv
                gain_back = gain[q, :, lanes] * bin_[q, rows, lanes].astype(f32)
                acc = acc + fold(scaled * gain_back)
            return acc

        acc = lax.fori_loop(0, NF, project, jnp.zeros((PR, 128), f32))
        mean = jnp.sum(acc, axis=1, keepdims=True) * (1.0 / D)
        for q in range(NF):
            owner = fsdp_peer(q) if q else f
            for s in range(COLS // SLAB):
                lanes = pl.ds(s * SLAB, SLAB)
                scaled = tok[q, rows, lanes].astype(f32) * inv
                gain_back = gain[q, :, lanes] * bin_[q, rows, lanes].astype(f32)
                out = pl.ds(pl.multiple_of(owner * COLS + s * SLAB, SLAB), SLAB)
                input_grad[rows, out] = (inv * (gain_back - scaled * mean)).astype(bf16)

    def x_scatter(k):
        return [
            remote(
                frag_in.at[
                    0,
                    pl.ds(pl.multiple_of(((x + d) % NX) * XB, XB), XB),
                    pl.ds(k * KC, KC),
                ],
                xr.at[k, d - 1],
                x_peer(d),
            )
            for d in range(1, NX)
        ]

    def x_sum(k):
        lanes = pl.ds(k * KC, KC)
        for h in range(NH):
            first = ((yh + h) % NH) * (NZ * SHARE)

            def one(zi, _):
                at = first + zi * SHARE
                own = pl.ds(pl.multiple_of(x * XB + at, SHARE), SHARE)
                rows = pl.ds(pl.multiple_of(at, SHARE), SHARE)
                total = frag[own, lanes].astype(f32)
                for d in range(NX - 1):
                    total = total + xr[k, d, rows, :].astype(f32)
                s1[k, zi, h] = total
                s1_sent[k, zi, h] = total.astype(bf16)
                return 0

            lax.fori_loop(0, NZ, one, 0)

    def z_scatter(k):
        return [
            remote(s1_sent.at[k, (z + d) % NZ], zr.at[k, d - 1], z_peer(d)) for d in range(1, NZ)
        ]

    def z_sum(k):
        total = s1[k, z]
        for d in range(NZ - 1):
            total = total + zr[k, d].astype(f32)
        s2[k] = total.astype(bf16)

    pull = outer_rate * (1.0 + momentum_decay)

    def outer_base():
        g = glob[...]
        base[0] = g - (pull * g + (outer_rate * momentum_decay**2) * moment[...])
        return remote(base.at[0], base.at[1], y_peer)

    def y_swap(k):
        return remote(s2.at[k], yr.at[k], y_peer)

    def update(k):
        lanes = pl.ds(k * KC, KC)
        for h in range(NH):
            mean = (s2[k, h].astype(f32) + yr[k, 1 - h].astype(f32)) * (1.0 / REPLICAS)
            gx[0, k, 0, h] = (base[h, :, lanes] + pull * mean).astype(bf16)
            if h == 0:
                g = glob[:, lanes]
                outer_grad = g - mean
                m = momentum_decay * moment[:, lanes] + outer_grad
                moment_new[0, :, lanes] = m
                global_new[0, :, lanes] = g - outer_rate * (outer_grad + momentum_decay * m)

    def z_gather(k):
        return [remote(gx.at[0, k, 0], gx.at[0, k, d], z_peer(d)) for d in range(1, NZ)]

    def x_gather(k):
        return [remote(gx.at[0, k], gx.at[e, k], x_peer(e)) for e in range(1, NX)]

    def mix(k, e):
        lanes = pl.ds(k * KC, KC)
        xi = (x + NX - e) % NX
        for h in range(NH):
            first = xi * XB + ((yh + h) % NH) * (NZ * SHARE)

            def one(d, _):
                at = first + ((z + NZ - d) % NZ) * SHARE
                rows = pl.ds(pl.multiple_of(at, SHARE), SHARE)
                mixed[0, rows, lanes] = (
                    mix_keep * frag[rows, lanes].astype(f32)
                    + (1.0 - mix_keep) * gx[e, k, d, h].astype(f32)
                ).astype(bf16)
                return 0

            lax.fori_loop(0, NZ, one, 0)

    def arrive(group):
        for copy in group if isinstance(group, list) else [group]:
            copy.wait_recv()

    live = {}

    def normed(c):
        normalise(c)
        live["nr", c] = send_block(nout, nin, n_relay_buf, c, 3)
        live["nl", c] = send_block(nout, nin, n_relay_buf, c, 1)

    def y_normed(c):
        live["nc", c] = send_block(nout, nin, n_relay_buf, c, 2)

    def pass_normed(c):
        live["np", c] = pass_on(nin, n_relay_buf, c, live["nr", c])

    def cot_on(_):
        arrive(live["cot2", 0])
        live["cot3", 0] = remote(cot.at[2], cot.at[3], f_peer[1])

    def back(_):
        load_cot.wait()
        load_weight.wait()
        arrive([live["cot1", 0], live["cot3", 0]])
        back_products()
        for c in range(PARTS):
            live["br", c] = send_block(bout, bin_, b_relay_buf, c, 3)
            live["bl", c] = send_block(bout, bin_, b_relay_buf, c, 1)

    def y_back(c):
        live["bc", c] = send_block(bout, bin_, b_relay_buf, c, 2)

    def pass_back(c):
        live["bp", c] = pass_on(bin_, b_relay_buf, c, live["br", c])

    def on_x(k):
        arrive(live["x", k])
        if k == 0:
            load_frag.wait()
        x_sum(k)
        if k == 0:
            enter_far()
            for copy in load_outer:
                copy.wait()
            live["base", 0] = outer_base()
        live["z", k] = z_scatter(k)

    def on_z(k):
        arrive(live["z", k])
        z_sum(k)
        live["y", k] = y_swap(k)

    def on_y(k):
        if k == 0:
            arrive(live["base", 0])
        arrive(live["y", k])
        update(k)
        live["zg", k] = z_gather(k)

    def on_zg(k):
        arrive(live["zg", k])
        live["xg", k] = x_gather(k)

    def on_xg(k):
        arrive(live["xg", k])
        for e in range(1, NX):
            mix(k, e)

    def keys(_):
        arrive([live[n, c] for n in ("nl", "nc", "np") for c in range(PARTS)])
        key_products()
        live["k3", 0] = remote(kp.at[3], kx, f_peer[1])
        live["k1", 0] = remote(kp.at[1], kp1, f_peer[1])

    def keys_on(_):
        arrive(live["k3", 0])
        ksend[...] = (FACTOR * (kp[2] + kx[...])).astype(bf16)
        live["k2", 0] = remote(ksend, kc, f_peer[2])

    def keys_out(_):
        arrive([live["k1", 0], live["k2", 0]])
        key_out[...] = (FACTOR * (kp[0] + kp1[...]) + kc[...].astype(f32)).astype(bf16)

    def tokens_out(c):
        arrive([live[n, c] for n in ("bl", "bc", "bp")])
        finish_tokens(c)

    steps = {
        "N": normed,
        "n": y_normed,
        "f": pass_normed,
        "C": cot_on,
        "Q": lambda _: hear_far(),
        "B": back,
        "b": y_back,
        "g": pass_back,
        "X": on_x,
        "Z": on_z,
        "Y": on_y,
        "V": on_zg,
        "E": on_xg,
        "K": keys,
        "L": keys_on,
        "H": keys_out,
        "W": lambda _: weight_products(),
        "M": lambda k: mix(k, 0),
        "F": tokens_out,
    }

    enter_near()
    live["cot2", 0] = remote(cot_in, cot.at[2], f_peer[2])
    for k in range(K):
        live["x", k] = x_scatter(k)
    for copy in load_tok + load_gain:
        copy.wait()
    normalise(0)
    y_normed(0)
    normalise(1)
    enter_chip()
    for c in range(2):
        live["nr", c] = send_block(nout, nin, n_relay_buf, c, 3)
        live["nl", c] = send_block(nout, nin, n_relay_buf, c, 1)
    live["cot1", 0] = remote(cot_in, cot.at[1], f_peer[1])
    for step in SCHEDULE:
        steps[step[0]](int(step[1:]))
    for copy in copies:
        copy.wait_send()


def write_out(*refs):
    sources, targets, sem = refs[:6], refs[6:12], refs[12]
    copies = [
        pltpu.make_async_copy(s, t, sem.at[i])
        for i, (s, t) in enumerate(zip(sources, targets, strict=True))
    ]
    for copy in copies:
        copy.start()
    for copy in copies:
        copy.wait()


def local(
    tokens, norm_gain, key_weight, key_cotangent, fragment_local, fragment_global, outer_moment
):
    hbm = pl.BlockSpec(memory_space=pltpu.HBM)
    vmem = pl.BlockSpec(memory_space=pltpu.VMEM)
    shapes = (
        jax.ShapeDtypeStruct((TOK, KV), bf16),
        jax.ShapeDtypeStruct((TOK, D), bf16),
        jax.ShapeDtypeStruct((1, COLS, KV), bf16),
        jax.ShapeDtypeStruct((1, COLS, KV), bf16),
        jax.ShapeDtypeStruct((1, SHARE, KV), f32),
        jax.ShapeDtypeStruct((1, SHARE, KV), f32),
    )
    results = pl.pallas_call(
        kernel,
        name="diloco_step",
        out_shape=shapes,
        in_specs=[hbm] * 7,
        out_specs=(vmem,) * 6,
        scratch_shapes=[
            pltpu.VMEM((NF, TOK, COLS), bf16),
            pltpu.VMEM((NF, 1, COLS), f32),
            pltpu.VMEM((COLS, KV), bf16),
            pltpu.VMEM((COLS, KV), bf16),
            pltpu.VMEM((SHARE, KV), f32),
            pltpu.VMEM((SHARE, KV), f32),
            pltpu.VMEM((NF, TOK, KV), bf16),
            pltpu.VMEM((NF, TOK, COLS), bf16),
            pltpu.VMEM((NF, TOK, COLS), bf16),
            pltpu.VMEM((TOK, COLS), bf16),
            pltpu.VMEM((TOK, COLS), bf16),
            pltpu.VMEM((TOK, 128), f32),
            pltpu.VMEM((NF, TOK, COLS), bf16),
            pltpu.VMEM((NF, TOK, COLS), bf16),
            pltpu.VMEM((NF, TOK, KV), f32),
            pltpu.VMEM((TOK, KV), f32),
            pltpu.VMEM((TOK, KV), f32),
            pltpu.VMEM((TOK, KV), bf16),
            pltpu.VMEM((TOK, KV), bf16),
            pltpu.VMEM((K, NX - 1, XB, KC), bf16),
            pltpu.VMEM((K, NZ, NH, SHARE, KC), f32),
            pltpu.VMEM((K, NZ, NH, SHARE, KC), bf16),
            pltpu.VMEM((K, NZ - 1, NH, SHARE, KC), bf16),
            pltpu.VMEM((K, NH, SHARE, KC), bf16),
            pltpu.VMEM((K, NH, SHARE, KC), bf16),
            pltpu.VMEM((NH, SHARE, KV), f32),
            pltpu.VMEM((NX, K, NZ, NH, SHARE, KC), bf16),
            pltpu.SemaphoreType.DMA((N_COPIES,)),
            pltpu.SemaphoreType.DMA((N_COPIES,)),
            pltpu.SemaphoreType.DMA((N_LOADS,)),
            pltpu.SemaphoreType.REGULAR,
            pltpu.SemaphoreType.REGULAR,
        ],
        compiler_params=pltpu.CompilerParams(
            collective_id=0, has_side_effects=True, vmem_limit_bytes=36 << 20
        ),
    )(
        *(
            pltpu.with_memory_space_constraint(a, pltpu.HBM)
            for a in (
                tokens,
                norm_gain[None],
                key_weight,
                key_cotangent,
                fragment_local,
                fragment_global,
                outer_moment,
            )
        )
    )
    return pl.pallas_call(
        write_out,
        name="write_out",
        out_shape=shapes,
        in_specs=[vmem] * 6,
        out_specs=(hbm,) * 6,
        scratch_shapes=[pltpu.SemaphoreType.DMA((6,))],
        compiler_params=pltpu.CompilerParams(vmem_limit_bytes=1 << 20),
    )(*results)


def solution(mesh):
    return jax.shard_map(
        local,
        mesh=mesh,
        in_specs=(
            P(("replica", "fsdp"), None),
            P(),
            P("replica", "fsdp", None),
            P(("replica", "fsdp"), None),
            P("replica", "fsdp", None),
            P("fsdp", "replica", None),
            P("fsdp", "replica", None),
        ),
        out_specs=(
            P(("replica", "fsdp"), None),
            P(("replica", "fsdp"), None),
            P("replica", "fsdp", None),
            P("replica", "fsdp", None),
            P("fsdp", "replica", None),
            P("fsdp", "replica", None),
        ),
        check_vma=False,
    )
```
